256 devices in a mesh: slab: 8 (over z), sub: 32 (over x, y, core).
Axes of the slice: x: 4, y: 4, z: 8, core: 2. Of those that a mesh axis runs over, the one named last changes fastest.
Arguments:
- right_side: float32 [1280, 384, 128], P(('slab', 'sub')), may hold values from -12 to 12
- diag_tiles: bfloat16 [1280, 384, 384], P(('slab', 'sub')), may hold values from -0.25 to 4.75, as said below
- couple_tiles: bfloat16 [1280, 3, 384, 384], P(('slab', 'sub')), may hold values from -0.109375 to 0.109375
- deep_tiles: bfloat16 [1280, 384, 384], P(('slab', 'sub')), may hold values from -0.109375 to 0.109375
- peer_col: int32 [1280, 3], P(('slab', 'sub')), may hold values from 0 to 31, all different within a row; in each aligned block of 5 rows (0 to 4, 5 to 9, ...) no two rows name the same one
- peer_tile: int32 [1280, 3], P(('slab', 'sub')), may hold values from 0 to 4
- deep_tile: int32 [1280], P(('slab', 'sub')), may hold values from 0 to 4
Outputs:
- solution: float32 [1280, 384, 128], P(('slab', 'sub'))
- residual: float32 [1280, 384, 128], P(('slab', 'sub'))
The draws below stay inside these ranges and needn't reach their ends.
Inputs may be any that keep to these rules, and one draw needn't show every extreme that they name: `peer_col`: each row names 3 different subdomains; among the row tiles of one device no subdomain is named by more than 1 couplings, and that bound is reached on some device. `diag_tiles`: each diagonal tile is symmetric.
All inputs are finite; a program needn't handle non-finite values.
Results may differ from the reference program's by a relative error of at most 0.012.
Values may be sent and summed in bfloat16 or wider, within the bound.
No kernel may reach another device: no remote copies, remote signals or barrier semaphores. Data moves between devices by JAX's collectives and lax.ppermute only.
A program may use at most 128 MiB of HBM per device.

```python
import math
import jax
import jax.numpy as jnp
import numpy as np
from jax import lax

TD = 384
NV = 128
RT = 5
K = 3
CHEB = 3
CAP = 1
TILES = 1280
N_SLAB = 8
N_SUB = 32


def draw_diag_tiles(key, part):
    key = jax.random.fold_in(key, 11)
    noise_key, centre_key = jax.random.split(key)
    noise = jax.random.truncated_normal(noise_key, -4.0, 4.0, (TILES, TD, TD), jnp.float32)
    centre = jnp.exp(jax.random.uniform(centre_key, (TILES, TD, 1), jnp.float32, jnp.log(2.5), jnp.log(4.5)))
    symmetric = (noise + jnp.swapaxes(noise, 1, 2)) * 0.014
    identity = (jnp.arange(TD)[:, None] == jnp.arange(TD)[None, :]).astype(jnp.float32)
    return (symmetric + identity[None, :, :] * centre).astype(jnp.bfloat16)


def with_ends(values, key, low, top_value):
    shape = values.shape
    place = [jax.random.randint(jax.random.fold_in(key, axis), (), 0, shape[axis]) for axis in range(len(shape))]
    values = values.at[tuple(place)].set(low)
    longest = shape.index(max(shape))
    place[longest] = (place[longest] + 1) % shape[longest]
    return values.at[tuple(place)].set(top_value)


def level_of(own_key, shape, cuts, least, largest):
    loudness = 1.0
    for position, blocks in cuts:
        draws = jax.random.uniform(jax.random.fold_in(jax.random.fold_in(own_key, 6), position), (blocks,), jnp.float32, least / len(cuts), largest / len(cuts))
        loudness = loudness * jnp.repeat(jnp.exp(draws), shape[position] // blocks).reshape((-1,) + (1,) * (len(shape) - 1 - position))
    return loudness


def shared_out(own_key, own, number, rows, number_of, top, bound, skew):
    ranking = jax.random.permutation(own_key, number_of)
    heavy_load, ordinary = shares(number_of, rows * top, bound, skew, True), shares(number_of, rows * top, bound, skew, False)
    places = jnp.arange(number_of)

    def named(sizes, offset_by):
        used = int((sizes > 0).sum())
        fixed = max(1, used // 4)
        passed = fixed + (places - fixed + offset_by * (used - fixed)) % max(1, number_of - fixed)
        return jnp.zeros((number_of,), jnp.int32).at[ranking[jnp.where(places < fixed, places, passed)]].set(jnp.asarray(sizes, jnp.int32))

    sizes = jnp.where(number % 4 == 0, named(heavy_load, number // 4), named(ordinary, number - number // 4 - 1))
    mixed = jax.random.permutation(jax.random.fold_in(own, 3), number_of)
    source_of, receiver = mixed[0:number_of // 2 * 2:2], mixed[1:number_of // 2 * 2:2]
    room = jnp.minimum(sizes[source_of] - 1, bound - sizes[receiver]) // 2
    room = jnp.where((source_of == ranking[0]) | (receiver == ranking[0]) | (sizes[receiver] == 0), 0, jnp.maximum(room, 0))
    passed = jax.random.randint(jax.random.fold_in(own, 4), (number_of // 2,), 0, 1 << 20) % (room + 1)
    sizes = sizes.at[source_of].add(-passed).at[receiver].add(passed)
    members = jnp.searchsorted(jnp.cumsum(sizes), jnp.arange(rows * top), side="right").astype(jnp.int32)
    table = members.reshape(top, rows).T
    table = table[jax.random.permutation(jax.random.fold_in(own, 1), rows)]
    offset_by = jax.random.randint(jax.random.fold_in(own, 2), (rows, 1), 0, top)
    return jnp.take_along_axis(table, (jnp.arange(top)[None, :] + offset_by) % top, axis=1)


def shares(count, total, most, lean, full):
    weights = [(1 << 20) // math.isqrt(standing ** lean) + 1 for standing in range(1, count + 1)]
    largest = most if full else min(most, max(-(-total // count), total * weights[0] // sum(weights)))
    least = 1 if total - largest >= count - 1 else 0
    counts, rest = [largest] + [least] * (count - 1), total - largest - least * (count - 1)
    while rest > 0:
        movable = [i for i in range(1, count) if counts[i] < largest] or [i for i in range(1, count) if counts[i] < most]
        pool, budget = sum([weights[i] for i in movable]), rest
        for i in movable:
            extra = min(most - counts[i], max(1, budget * weights[i] // pool), rest)
            counts[i] = counts[i] + extra
            rest = rest - extra
    return np.array(counts)


def centred(stream_key, dims, deviation, most, cuts=(), kind=jnp.bfloat16):
    drawn = jax.random.normal(stream_key, dims, jnp.float32) * deviation
    if len(cuts) > 0:
        drawn = level_of(stream_key, dims, cuts, -0.22, 0.18) * drawn
    return jnp.clip(drawn, min=-most, max=most).astype(kind)


def setup_inputs(seed: int = 0) -> dict:
    key_of = jax.random.split(jax.random.key(seed), 8)
    right_side = centred(key_of[0], (TILES, TD, NV), 2.0, 12.0, ((0, 256),), jnp.float32)
    diag_tiles = draw_diag_tiles(jax.random.fold_in(key_of[7], 71), 0)
    couple_tiles = centred(key_of[2], (TILES, K, TD, TD), (8 * TD) ** -0.5, 0.109375, ((0, 256),))
    deep_tiles = centred(key_of[3], (TILES, TD, TD), (8 * TD) ** -0.5, 0.109375, ((0, 256),))
    peer_col_keys = jax.random.split(jax.random.fold_in(key_of[4], 1), TILES // RT)
    peer_col_turns = jax.random.permutation(jax.random.fold_in(key_of[4], 3), TILES // RT)
    peer_col = jax.vmap(lambda own, number: shared_out(jax.random.fold_in(key_of[4], 2), own, number, RT, N_SUB, K, CAP, 2))(peer_col_keys, peer_col_turns).reshape((TILES, K))
    peer_tile = with_ends(jax.random.randint(key_of[5], (TILES, K), 0, RT), jax.random.fold_in(key_of[5], 1), 0, RT - 1).astype(jnp.int32)
    deep_tile = with_ends(jax.random.randint(key_of[6], (TILES,), 0, RT), jax.random.fold_in(key_of[6], 1), 0, RT - 1).astype(jnp.int32)
    return dict(right_side=right_side, diag_tiles=diag_tiles, couple_tiles=couple_tiles, deep_tiles=deep_tiles, peer_col=peer_col, peer_tile=peer_tile, deep_tile=deep_tile)


spectrum_low = 0.5
spectrum_high = 6.5


def to_half(values):
    return lax.optimization_barrier(values.astype(jnp.bfloat16)).astype(jnp.float32)


def apply_matrix(dir_half, diag_tiles, couple_tiles, deep_tiles, far_col, deep_col, deep_live):
    def sweep_device(accum, device):
        start = (device * RT).astype(jnp.int32)
        local = lax.dynamic_slice_in_dim(dir_half, start, RT, 0).astype(jnp.float32)
        diag_part = lax.dynamic_slice_in_dim(diag_tiles, start, RT, 0).astype(jnp.float32)
        couple_part = lax.dynamic_slice_in_dim(couple_tiles, start, RT, 0).astype(jnp.float32)
        deep_part = lax.dynamic_slice_in_dim(deep_tiles, start, RT, 0).astype(jnp.float32)
        columns = lax.dynamic_slice_in_dim(far_col, start, RT, 0)
        deep_cols = lax.dynamic_slice_in_dim(deep_col, start, RT, 0)
        live_rows = lax.dynamic_slice_in_dim(deep_live, start, RT, 0)[:, None, None]
        reached = dir_half[columns].astype(jnp.float32)
        deep_reached = dir_half[deep_cols].astype(jnp.float32)
        direct = jnp.einsum("tab,tbn->tan", diag_part, local)
        direct = direct + jnp.einsum("tkab,tkbn->tan", couple_part, reached)
        direct = direct + jnp.einsum("tab,tbn->tan", deep_part, deep_reached) * live_rows
        transposed = to_half(jnp.einsum("tkab,tan->tkbn", couple_part, local))
        deep_back = to_half(jnp.einsum("tab,tan->tbn", deep_part, local)) * live_rows
        accum = accum.at[columns.reshape(-1)].add(transposed.reshape(RT * K, TD, NV))
        accum = accum.at[deep_cols].add(deep_back)
        block = lax.dynamic_slice_in_dim(accum, start, RT, 0) + direct
        accum = lax.dynamic_update_slice_in_dim(accum, block, start, 0)
        return accum, None

    accum, unused = lax.scan(sweep_device, jnp.zeros(dir_half.shape, jnp.float32), jnp.arange(N_SLAB * N_SUB, dtype=jnp.int32))
    return accum


def reference(right_side, diag_tiles, couple_tiles, deep_tiles, peer_col, peer_tile, deep_tile):
    tile_ids = jnp.arange(TILES, dtype=jnp.int32)
    device = tile_ids // RT
    slab_index = device // N_SUB
    far_col = (RT * (N_SUB * slab_index[:, None] + peer_col) + peer_tile).astype(jnp.int32)
    deep_col = jnp.minimum(RT * (device + N_SUB) + deep_tile, TILES - 1).astype(jnp.int32)
    deep_live = (slab_index < N_SLAB - 1).astype(jnp.float32)
    centre = 0.5 * (spectrum_high + spectrum_low)
    spread = 0.5 * (spectrum_high - spectrum_low)
    sigma_ratio = centre / spread
    solution = jnp.zeros(right_side.shape, jnp.float32)
    residual = right_side
    direction = right_side / centre
    rho_prev = 1.0 / sigma_ratio
    for sweep in range(CHEB):
        solution = solution + direction
        dir_half = direction.astype(jnp.bfloat16)
        residual = residual - apply_matrix(dir_half, diag_tiles, couple_tiles, deep_tiles, far_col, deep_col, deep_live)
        if sweep + 1 < CHEB:
            rho_next = 1.0 / (2.0 * sigma_ratio - rho_prev)
            direction = rho_next * rho_prev * direction + (2.0 * rho_next / spread) * residual
            rho_prev = rho_next
    return solution, residual
```

```python
import jax
import jax.numpy as jnp
from jax import lax
from jax.experimental import pallas as pl
from jax.experimental.pallas import tpu as pltpu
from jax.sharding import PartitionSpec as P

CHEB = 3
NX = 4
NY = 4
RT = 5
K = 3
REFS = RT * K
TD = 384
NV = 128
NSUB = 32
AT_X, AT_Y, AT_C, AT_DEEP = REFS, REFS + 1, REFS + 2, REFS + 3

spectrum_low = 0.5
spectrum_high = 6.5


def place(x, y, c):
    return ((x % NX) * NY + (y % NY)) * 2 + c


EVERY = [(x, y, c) for x in range(NX) for y in range(NY) for c in range(2)]


def first_axis(e):
    return [(place(x, y, c), place(x, y + e, 0) if c == 0 else place(x + e, y, 1)) for x, y, c in EVERY]


def second_same(e):
    return [(place(x, y, c), place(x + e, y, 0) if c == 0 else place(x, y + e, 1)) for x, y, c in EVERY]


def relay_to_cross(e):
    return [(place(x, y, c), place(x + e, y, 1) if c == 0 else place(x, y + e, 0)) for x, y, c in EVERY]


def cross_to_relay(e):
    return [(place(x, y, c), place(x, y + e, 1) if c == 0 else place(x + e, y, 0)) for x, y, c in EVERY]


def from_behind(value, axis, by):
    devices = lax.axis_size(axis)
    pairs = [(i, i + by) for i in range(devices) if 0 <= i + by < devices]
    return lax.ppermute(value, axis, pairs)


def peer_place(info, i):
    q = info[i]
    qx, qy, qc = q >> 3, (q >> 1) & 3, q & 1
    even = qc == 0
    step = jnp.where(even, qx - info[AT_X], qy - info[AT_Y]) & 3
    slot = jnp.where(even, qy, qx)
    rel = jnp.where(qc == info[AT_C], 0, 4)
    return rel, step, slot


def along(info):
    return jnp.where(info[AT_C] == 0, info[AT_Y], info[AT_X])


def asked(info, table, rel, step, slot):
    x, y, c = info[AT_X], info[AT_Y], info[AT_C]
    even = c == 0
    px = jnp.where(even, (x + step) & 3, x)
    py = jnp.where(even, y, (y + step) & 3)
    pc = c ^ 1 if rel else c
    ox = jnp.where(even, x, slot)
    oy = jnp.where(even, slot, y)
    return table[((px * NY + py) * 2 + pc) * NSUB + (ox * NY + oy) * 2 + c] - 1


def products_kernel(info, d_ref, couple_ref, deep_ref, *rest):
    outs, back_ref, acc = rest[:8], rest[8], rest[9]
    s = pl.program_id(0)
    d = d_ref[0]

    @pl.when(s == 0)
    def _():
        acc[...] = jnp.zeros_like(acc)

    for k in range(K):
        rel, step, slot = peer_place(info, s * K + k)
        group = rel + step
        prod = jnp.dot(d, couple_ref[0, k], preferred_element_type=jnp.float32).astype(jnp.bfloat16)
        for g in range(8):

            @pl.when(group == g)
            def _(g=g, prod=prod, slot=slot):
                outs[g][slot] = prod

    target = info[AT_DEEP + s]
    acc[target] += jnp.dot(d, deep_ref[0], preferred_element_type=jnp.float32)

    @pl.when(s == RT - 1)
    def _():
        back_ref[...] = acc[...].astype(jnp.bfloat16)


def pack_kernel(info, table, *rest):
    lines, outs = rest[:4], rest[4:]
    u = along(info)
    for g in range(8):
        for e in range(4):
            slot = (u - e) & 3
            tile = asked(info, table, g >= 4, g & 3, slot)

            @pl.when(tile >= 0)
            def _(g=g, e=e, slot=slot, tile=tile):
                outs[g][slot] = lines[e][tile]


def combine_kernel(info, table, *rest):
    groups, outs, acc = rest[:8], rest[8:12], rest[12]
    step = pl.program_id(0)
    slot = (along(info) + step) & 3
    acc[...] = jnp.zeros_like(acc)
    for g in range(8):
        tile = asked(info, table, g >= 4, -(g & 3), slot)

        @pl.when(tile >= 0)
        def _(g=g, tile=tile):
            acc[tile] += groups[g][0].astype(jnp.float32)

    for e in range(4):

        @pl.when(step == e)
        def _(e=e):
            outs[e][...] = acc[...].astype(jnp.bfloat16)


def direct_kernel(info, d_ref, diag_ref, couple_ref, deep_ref, deeper_ref, *rest):
    groups, out_ref, got = rest[:8], rest[8], rest[9]
    s = pl.program_id(0)
    for k in range(K):
        rel, step, slot = peer_place(info, s * K + k)
        group = rel + ((-step) & 3)
        for g in range(8):

            @pl.when(group == g)
            def _(g=g, k=k, slot=slot):
                got[k] = groups[g][slot]

    nt = (((1,), (1,)), ((), ()))
    total = lax.dot_general(d_ref[0], diag_ref[0], nt, preferred_element_type=jnp.float32)
    total += lax.dot_general(
        deeper_ref[info[AT_DEEP + s]], deep_ref[0], nt, preferred_element_type=jnp.float32
    )
    for k in range(K):
        total += lax.dot_general(got[k], couple_ref[0, k], nt, preferred_element_type=jnp.float32)
    out_ref[0] = total


def whole(shape):
    return pl.BlockSpec(shape, lambda *a: (0,) * len(shape))


def row(shape):
    return pl.BlockSpec(shape, lambda s, *a: (s,) + (0,) * (len(shape) - 1))


PARAMS = dict(vmem_limit_bytes=32 * 1024 * 1024)
GROUP = (4, NV, TD)
LINE = (RT, NV, TD)


def bf(shape):
    return jax.ShapeDtypeStruct(shape, jnp.bfloat16)


def products(info, d, couple, deep):
    return pl.pallas_call(
        products_kernel,
        grid_spec=pltpu.PrefetchScalarGridSpec(
            num_scalar_prefetch=1,
            grid=(RT,),
            in_specs=[row((1, NV, TD)), row((1, K, TD, TD)), row((1, TD, TD))],
            out_specs=[whole(GROUP)] * 8 + [whole(LINE)],
            scratch_shapes=[pltpu.VMEM(LINE, jnp.float32)],
        ),
        out_shape=[bf(GROUP)] * 8 + [bf(LINE)],
        compiler_params=pltpu.CompilerParams(**PARAMS),
        cost_estimate=pl.CostEstimate(flops=20 * 2 * NV * TD * TD, bytes_accessed=10_000_000, transcendentals=0),
        name="products",
    )(info, d, couple, deep)


def pack(info, table, lines):
    return pl.pallas_call(
        pack_kernel,
        grid_spec=pltpu.PrefetchScalarGridSpec(
            num_scalar_prefetch=2,
            grid=(1,),
            in_specs=[whole(LINE)] * 4,
            out_specs=[whole(GROUP)] * 8,
        ),
        out_shape=[bf(GROUP)] * 8,
        compiler_params=pltpu.CompilerParams(**PARAMS),
        cost_estimate=pl.CostEstimate(flops=0, bytes_accessed=5_000_000, transcendentals=0),
        name="pack",
    )(info, table, *lines)


def combine(info, table, groups):
    def at(step, info, table):
        return ((along(info) + step) & 3, 0, 0)

    return pl.pallas_call(
        combine_kernel,
        grid_spec=pltpu.PrefetchScalarGridSpec(
            num_scalar_prefetch=2,
            grid=(4,),
            in_specs=[pl.BlockSpec((1, NV, TD), at)] * 8,
            out_specs=[whole(LINE)] * 4,
            scratch_shapes=[pltpu.VMEM(LINE, jnp.float32)],
        ),
        out_shape=[bf(LINE)] * 4,
        compiler_params=pltpu.CompilerParams(**PARAMS),
        cost_estimate=pl.CostEstimate(flops=2_000_000, bytes_accessed=8_000_000, transcendentals=0),
        name="combine",
    )(info, table, *groups)


def direct(info, d, diag, couple, deep, deeper, groups):
    return pl.pallas_call(
        direct_kernel,
        grid_spec=pltpu.PrefetchScalarGridSpec(
            num_scalar_prefetch=1,
            grid=(RT,),
            in_specs=[
                row((1, NV, TD)),
                row((1, TD, TD)),
                row((1, K, TD, TD)),
                row((1, TD, TD)),
                whole(LINE),
            ]
            + [whole(GROUP)] * 8,
            out_specs=row((1, NV, TD)),
            scratch_shapes=[pltpu.VMEM((K, NV, TD), jnp.bfloat16)],
        ),
        out_shape=jax.ShapeDtypeStruct(LINE, jnp.float32),
        compiler_params=pltpu.CompilerParams(**PARAMS),
        cost_estimate=pl.CostEstimate(flops=25 * 2 * NV * TD * TD, bytes_accessed=12_000_000, transcendentals=0),
        name="direct",
    )(info, d, diag, couple, deep, deeper, *groups)


def local(right_side, diag_tiles, couple_tiles, deep_tiles, peer_col, peer_tile, deep_tile):
    me = lax.axis_index("sub").astype(jnp.int32)
    flat_peer = peer_col.reshape(REFS)
    flat_tile = peer_tile.reshape(REFS)
    coords = jnp.stack([me >> 3, (me >> 1) & 3, me & 1])
    info = jnp.concatenate([flat_peer, coords, deep_tile])
    names = flat_peer[:, None] == jnp.arange(NSUB, dtype=jnp.int32)[None, :]
    want = jnp.sum(jnp.where(names, flat_tile[:, None] + 1, 0), axis=0)
    table = lax.all_to_all(
        jnp.broadcast_to(want[None, :], (NSUB, NSUB)), "sub", split_axis=0, concat_axis=0, tiled=True
    ).reshape(NSUB * NSUB)

    centre = 0.5 * (spectrum_high + spectrum_low)
    spread = 0.5 * (spectrum_high - spectrum_low)
    sigma_ratio = centre / spread
    residual = jnp.swapaxes(right_side, 1, 2)
    direction = residual / centre
    solution = direction
    rho_prev = 1.0 / sigma_ratio
    for sweep in range(CHEB):
        d = direction.astype(jnp.bfloat16)
        lines = [d] + [lax.ppermute(d, "sub", first_axis(e)) for e in (1, 2, 3)]
        deeper = from_behind(d, "slab", -1)
        *sent, deep_back = products(info, d, couple_tiles, deep_tiles)
        deep_got = from_behind(deep_back, "slab", 1)
        backs = [sent[0]] + [lax.ppermute(sent[e], "sub", second_same(e)) for e in (1, 2, 3)]
        backs += [lax.ppermute(sent[4 + e], "sub", cross_to_relay(e)) for e in range(4)]
        packed = pack(info, table, lines)
        reached = [packed[0]] + [lax.ppermute(packed[e], "sub", second_same(e)) for e in (1, 2, 3)]
        reached += [lax.ppermute(packed[4 + e], "sub", relay_to_cross(e)) for e in range(4)]
        sums = combine(info, table, backs)
        owned = [sums[0]] + [lax.ppermute(sums[e], "sub", first_axis(e)) for e in (1, 2, 3)]
        accum = direct(info, d, diag_tiles, couple_tiles, deep_tiles, deeper, reached)
        for part in owned + [deep_got]:
            accum = accum + part.astype(jnp.float32)
        residual = residual - accum
        if sweep + 1 < CHEB:
            rho_next = 1.0 / (2.0 * sigma_ratio - rho_prev)
            direction = rho_next * rho_prev * direction + 2.0 * rho_next / spread * residual
            solution = solution + direction
            rho_prev = rho_next
    return (jnp.swapaxes(solution, 1, 2), jnp.swapaxes(residual, 1, 2))


def solution(mesh):
    return jax.shard_map(
        local,
        mesh=mesh,
        in_specs=(
            P(("slab", "sub"), None, None),
            P(("slab", "sub"), None, None),
            P(("slab", "sub"), None, None, None),
            P(("slab", "sub"), None, None),
            P(("slab", "sub"), None),
            P(("slab", "sub"), None),
            P(("slab", "sub")),
        ),
        out_specs=(P(("slab", "sub"), None, None), P(("slab", "sub"), None, None)),
        check_vma=False,
    )
```

```python
import functools

import jax
import jax.numpy as jnp
from jax import lax
from jax.experimental import pallas as pl
from jax.experimental.pallas import tpu as pltpu
from jax.sharding import PartitionSpec as P

CHEB = 3
NX = 4
NY = 4
RT = 5
K = 3
REFS = RT * K
TD = 384
NV = 128
NSUB = 32
AT_X, AT_Y, AT_C, AT_DEEP = REFS, REFS + 1, REFS + 2, REFS + 3

spectrum_low = 0.5
spectrum_high = 6.5


def place(x, y, c):
    return ((x % NX) * NY + (y % NY)) * 2 + c


EVERY = [(x, y, c) for x in range(NX) for y in range(NY) for c in range(2)]


def first_axis(e):
    return [(place(x, y, c), place(x, y + e, 0) if c == 0 else place(x + e, y, 1)) for x, y, c in EVERY]


def second_same(e):
    return [(place(x, y, c), place(x + e, y, 0) if c == 0 else place(x, y + e, 1)) for x, y, c in EVERY]


SWAP = [(place(x, y, c), place(x, y, 1 - c)) for x, y, c in EVERY]


def from_behind(value, axis, by):
    devices = lax.axis_size(axis)
    pairs = [(i, i + by) for i in range(devices) if 0 <= i + by < devices]
    return lax.ppermute(value, axis, pairs)


def peer_place(info, i):
    q = info[i]
    qx, qy, qc = q >> 3, (q >> 1) & 3, q & 1
    even = qc == 0
    step = jnp.where(even, qx - info[AT_X], qy - info[AT_Y]) & 3
    slot = jnp.where(even, qy, qx)
    rel = jnp.where(qc == info[AT_C], 0, 4)
    return rel, step, slot


def along(info):
    return jnp.where(info[AT_C] == 0, info[AT_Y], info[AT_X])


def asked(info, table, rel, step, slot):
    x, y, c = info[AT_X], info[AT_Y], info[AT_C]
    even = c == 0
    px = jnp.where(even, (x + step) & 3, x)
    py = jnp.where(even, y, (y + step) & 3)
    pc = c ^ 1 if rel else c
    ox = jnp.where(even, x, slot)
    oy = jnp.where(even, slot, y)
    return table[((px * NY + py) * 2 + pc) * NSUB + (ox * NY + oy) * 2 + c] - 1


def products_kernel(info, d_ref, couple_ref, own_ref, cross_ref, slots):
    s = pl.program_id(0)
    d = d_ref[0]
    prods = [jnp.dot(d, couple_ref[0, k], preferred_element_type=jnp.float32) for k in range(K)]
    for k in range(K):
        rel, step, slot = peer_place(info, s * K + k)
        slots[(rel + step) * 4 + slot] = prods[k].astype(jnp.bfloat16)

    @pl.when(s == RT - 1)
    def _():
        own_ref[...] = slots[:16]
        cross_ref[...] = slots[16:]


def dense_kernel(info, d_ref, diag_ref, deep_ref, base_ref, back_ref, acc):
    s = pl.program_id(0)

    @pl.when(s == 0)
    def _():
        acc[...] = jnp.zeros_like(acc)

    d = d_ref[0]
    base_ref[0] = lax.dot_general(d, diag_ref[0], NT, preferred_element_type=jnp.float32)
    acc[info[AT_DEEP + s]] += jnp.dot(d, deep_ref[0], preferred_element_type=jnp.float32)

    @pl.when(s == RT - 1)
    def _():
        back_ref[...] = acc[...].astype(jnp.bfloat16)


def pack_kernel(info, table, *rest):
    lines, outs = rest[:4], rest[4:]
    u = along(info)
    for step in range(4):
        for rel in range(2):
            out = outs[rel] if step == 0 else outs[step + 1]
            base = 4 * rel if step else 0
            for e in range(4):
                slot = (u - e) & 3
                tile = asked(info, table, rel, step, slot)

                @pl.when(tile >= 0)
                def _(out=out, base=base, e=e, slot=slot, tile=tile):
                    out[base + slot] = lines[e][tile]


def copies_kernel(moves, sources, *rest):
    refs, sem = rest[:-1], rest[-1]
    started = []
    for i, (src, at, dst, to, count) in enumerate(moves):
        copy = pltpu.make_async_copy(
            refs[src].at[at : at + count], refs[sources + dst].at[to : to + count], sem.at[i]
        )
        copy.start()
        started.append(copy)
    for copy in started:
        copy.wait()


def combine_kernel(info, table, *rest):
    groups, outs, acc = rest[:8], rest[8:12], rest[12]
    step = pl.program_id(0)
    slot = (along(info) + step) & 3
    acc[...] = jnp.zeros_like(acc)
    for e in range(4):
        for rel in range(2):
            tile = asked(info, table, rel, -e, slot)

            @pl.when(tile >= 0)
            def _(g=2 * e + rel, tile=tile):
                acc[tile] += groups[g][0].astype(jnp.float32)

    for e in range(4):

        @pl.when(step == e)
        def _(e=e):
            outs[e][...] = acc[...].astype(jnp.bfloat16)


def direct_kernel(info, base_ref, couple_ref, deep_ref, deeper_ref, *rest):
    groups, out_ref, slots = rest[:5], rest[5], rest[6]
    s = pl.program_id(0)

    @pl.when(s == 0)
    def _():
        for e in range(4):
            slots[4 * e : 4 * e + 4] = groups[e][...]
        slots[16:] = groups[4][...]

    total = base_ref[0] + lax.dot_general(
        deeper_ref[info[AT_DEEP + s]], deep_ref[0], NT, preferred_element_type=jnp.float32
    )
    for k in range(K):
        rel, step, slot = peer_place(info, s * K + k)
        got = slots[(rel + ((-step) & 3)) * 4 + slot]
        total += lax.dot_general(got, couple_ref[0, k], NT, preferred_element_type=jnp.float32)
    out_ref[0] = total


def whole(shape):
    return pl.BlockSpec(shape, lambda *a: (0,) * len(shape))


def row(shape):
    return pl.BlockSpec(shape, lambda s, *a: (s,) + (0,) * (len(shape) - 1))


PARAMS = dict(vmem_limit_bytes=20 * 1024 * 1024)
NT = (((1,), (1,)), ((), ()))
LONG = pl.CostEstimate(flops=50_000_000_000, bytes_accessed=100_000_000, transcendentals=0)
COST = pl.CostEstimate(flops=1000, bytes_accessed=1000, transcendentals=0)
GROUP = (4, NV, TD)
PAIR = (8, NV, TD)
HALF = (16, NV, TD)
LINE = (RT, NV, TD)


def bf(shape):
    return jax.ShapeDtypeStruct(shape, jnp.bfloat16)


def products(info, d, couple):
    return pl.pallas_call(
        products_kernel,
        grid_spec=pltpu.PrefetchScalarGridSpec(
            num_scalar_prefetch=1,
            grid=(RT,),
            in_specs=[row((1, NV, TD)), row((1, K, TD, TD))],
            out_specs=[whole(HALF)] * 2,
            scratch_shapes=[pltpu.VMEM((32, NV, TD), jnp.bfloat16)],
        ),
        out_shape=[bf(HALF)] * 2,
        compiler_params=pltpu.CompilerParams(**PARAMS),
        cost_estimate=COST,
        name="products",
    )(info, d, couple)


def dense(info, d, diag, deep):
    return pl.pallas_call(
        dense_kernel,
        grid_spec=pltpu.PrefetchScalarGridSpec(
            num_scalar_prefetch=1,
            grid=(RT,),
            in_specs=[row((1, NV, TD)), row((1, TD, TD)), row((1, TD, TD))],
            out_specs=[row((1, NV, TD)), whole(LINE)],
            scratch_shapes=[pltpu.VMEM(LINE, jnp.float32)],
        ),
        out_shape=[jax.ShapeDtypeStruct(LINE, jnp.float32), bf(LINE)],
        compiler_params=pltpu.CompilerParams(**PARAMS),
        cost_estimate=LONG,
        name="dense",
    )(info, d, diag, deep)


def pack(info, table, lines):
    return pl.pallas_call(
        pack_kernel,
        grid_spec=pltpu.PrefetchScalarGridSpec(
            num_scalar_prefetch=2,
            grid=(1,),
            in_specs=[whole(LINE)] * 4,
            out_specs=[whole(GROUP)] * 2 + [whole(PAIR)] * 3,
        ),
        out_shape=[bf(GROUP)] * 2 + [bf(PAIR)] * 3,
        compiler_params=pltpu.CompilerParams(**PARAMS),
        cost_estimate=COST,
        name="pack",
    )(info, table, *lines)


def copies(arrays, shapes, moves, name):
    anywhere = pl.BlockSpec(memory_space=pl.ANY)
    return pl.pallas_call(
        functools.partial(copies_kernel, moves, len(arrays)),
        in_specs=[anywhere] * len(arrays),
        out_specs=[anywhere] * len(shapes),
        out_shape=[bf(shape) for shape in shapes],
        scratch_shapes=[pltpu.SemaphoreType.DMA((len(moves),))],
        compiler_params=pltpu.CompilerParams(**PARAMS),
        cost_estimate=COST,
        name=name,
    )(*arrays)


def combine(info, table, own, cross, arrived):
    def at(base):
        return pl.BlockSpec(
            (1, NV, TD), lambda step, info, table: (base + ((along(info) + step) & 3), 0, 0)
        )

    args = [own, cross]
    for pair in arrived:
        args += [pair, pair]
    return pl.pallas_call(
        combine_kernel,
        grid_spec=pltpu.PrefetchScalarGridSpec(
            num_scalar_prefetch=2,
            grid=(4,),
            in_specs=[at(0), at(0)] + [at(0), at(4)] * 3,
            out_specs=[whole(LINE)] * 4,
            scratch_shapes=[pltpu.VMEM(LINE, jnp.float32)],
        ),
        out_shape=[bf(LINE)] * 4,
        compiler_params=pltpu.CompilerParams(**PARAMS),
        cost_estimate=COST,
        name="combine",
    )(info, table, *args)


def direct(info, base, couple, deep, deeper, groups):
    return pl.pallas_call(
        direct_kernel,
        grid_spec=pltpu.PrefetchScalarGridSpec(
            num_scalar_prefetch=1,
            grid=(RT,),
            in_specs=[
                row((1, NV, TD)),
                row((1, K, TD, TD)),
                row((1, TD, TD)),
                whole(LINE),
            ]
            + [whole(GROUP)] * 4
            + [whole(HALF)],
            out_specs=row((1, NV, TD)),
            scratch_shapes=[pltpu.VMEM((32, NV, TD), jnp.bfloat16)],
        ),
        out_shape=jax.ShapeDtypeStruct(LINE, jnp.float32),
        compiler_params=pltpu.CompilerParams(**PARAMS),
        cost_estimate=COST,
        name="direct",
    )(info, base, couple, deep, deeper, *groups)


def local(right_side, diag_tiles, couple_tiles, deep_tiles, peer_col, peer_tile, deep_tile):
    me = lax.axis_index("sub").astype(jnp.int32)
    flat_peer = peer_col.reshape(REFS)
    flat_tile = peer_tile.reshape(REFS)
    coords = jnp.stack([me >> 3, (me >> 1) & 3, me & 1])
    info = jnp.concatenate([flat_peer, coords, deep_tile])
    names = flat_peer[:, None] == jnp.arange(NSUB, dtype=jnp.int32)[None, :]
    want = jnp.sum(jnp.where(names, flat_tile[:, None] + 1, 0), axis=0)
    table = lax.all_to_all(
        jnp.broadcast_to(want[None, :], (NSUB, NSUB)), "sub", split_axis=0, concat_axis=0, tiled=True
    ).reshape(NSUB * NSUB)

    centre = 0.5 * (spectrum_high + spectrum_low)
    spread = 0.5 * (spectrum_high - spectrum_low)
    sigma_ratio = centre / spread
    residual = jnp.swapaxes(right_side, 1, 2)
    direction = residual / centre
    solution = direction
    rho_prev = 1.0 / sigma_ratio
    for sweep in range(CHEB):
        d = direction.astype(jnp.bfloat16)
        if sweep == 0:
            d, table = lax.optimization_barrier((d, table))
        lines = [d] + [lax.ppermute(d, "sub", first_axis(e)) for e in (1, 2, 3)]
        deeper = from_behind(d, "slab", -1)
        own, cross = products(info, d, couple_tiles)
        base, deep_back = dense(info, d, diag_tiles, deep_tiles)
        cross = lax.ppermute(cross, "sub", SWAP)
        deep_got = from_behind(deep_back, "slab", 1)
        joined = copies(
            [own, cross],
            [PAIR] * 3,
            [(s, 4 * e, e - 1, 4 * s, 4) for e in (1, 2, 3) for s in (0, 1)],
            "join",
        )
        arrived = [lax.ppermute(joined[e - 1], "sub", second_same(e)) for e in (1, 2, 3)]
        unused, lines[1:], deeper, base = lax.optimization_barrier((joined, lines[1:], deeper, base))
        near, over, *packed = pack(info, table, lines)
        reached = [lax.ppermute(packed[e - 1], "sub", second_same(e)) for e in (1, 2, 3)]
        sums = combine(info, table, own, cross, arrived)
        owned = [sums[0]] + [lax.ppermute(sums[e], "sub", first_axis(e)) for e in (1, 2, 3)]
        owned, reached, deep_got = lax.optimization_barrier((owned, reached, deep_got))
        (over,) = copies(
            [over] + reached, [HALF], [(e, 4 * (e > 0), 0, 4 * e, 4) for e in range(4)], "collect"
        )
        over = lax.ppermute(over, "sub", SWAP)
        accum = direct(info, base, couple_tiles, deep_tiles, deeper, [near] + reached + [over])
        for part in owned + [deep_got]:
            accum = accum + part.astype(jnp.float32)
        residual = residual - accum
        if sweep + 1 < CHEB:
            rho_next = 1.0 / (2.0 * sigma_ratio - rho_prev)
            direction = rho_next * rho_prev * direction + 2.0 * rho_next / spread * residual
            solution = solution + direction
            rho_prev = rho_next
    return (jnp.swapaxes(solution, 1, 2), jnp.swapaxes(residual, 1, 2))


def solution(mesh):
    return jax.shard_map(
        local,
        mesh=mesh,
        in_specs=(
            P(("slab", "sub"), None, None),
            P(("slab", "sub"), None, None),
            P(("slab", "sub"), None, None, None),
            P(("slab", "sub"), None, None),
            P(("slab", "sub"), None),
            P(("slab", "sub"), None),
            P(("slab", "sub")),
        ),
        out_specs=(P(("slab", "sub"), None, None), P(("slab", "sub"), None, None)),
        check_vma=False,
    )
```

```python
import functools

import jax
import jax.numpy as jnp
from jax import lax
from jax.experimental import pallas as pl
from jax.experimental.pallas import tpu as pltpu
from jax.sharding import PartitionSpec as P

CHEB = 3
NX = 4
NY = 4
RT = 5
K = 3
REFS = RT * K
TD = 384
NV = 128
NSUB = 32
AT_X, AT_Y, AT_C, AT_DEEP = REFS, REFS + 1, REFS + 2, REFS + 3

spectrum_low = 0.5
spectrum_high = 6.5


def place(x, y, c):
    return ((x % NX) * NY + (y % NY)) * 2 + c


EVERY = [(x, y, c) for x in range(NX) for y in range(NY) for c in range(2)]


def first_axis(e):
    return [(place(x, y, c), place(x, y + e, 0) if c == 0 else place(x + e, y, 1)) for x, y, c in EVERY]


def second_same(e):
    return [(place(x, y, c), place(x + e, y, 0) if c == 0 else place(x, y + e, 1)) for x, y, c in EVERY]


SWAP = [(place(x, y, c), place(x, y, 1 - c)) for x, y, c in EVERY]


def from_behind(value, axis, by):
    devices = lax.axis_size(axis)
    pairs = [(i, i + by) for i in range(devices) if 0 <= i + by < devices]
    return lax.ppermute(value, axis, pairs)


def peer_place(info, i):
    q = info[i]
    qx, qy, qc = q >> 3, (q >> 1) & 3, q & 1
    even = qc == 0
    step = jnp.where(even, qx - info[AT_X], qy - info[AT_Y]) & 3
    slot = jnp.where(even, qy, qx)
    rel = jnp.where(qc == info[AT_C], 0, 4)
    return rel, step, slot


def along(info):
    return jnp.where(info[AT_C] == 0, info[AT_Y], info[AT_X])


def asked(info, table, rel, step, slot):
    x, y, c = info[AT_X], info[AT_Y], info[AT_C]
    even = c == 0
    px = jnp.where(even, (x + step) & 3, x)
    py = jnp.where(even, y, (y + step) & 3)
    pc = c ^ 1 if rel else c
    ox = jnp.where(even, x, slot)
    oy = jnp.where(even, slot, y)
    return table[(px * NY + py) * 2 + pc, (ox * NY + oy) * 2 + c] - 1


def products_kernel(info, d_ref, couple_ref, own_ref, cross_ref, slots):
    s = pl.program_id(0)
    d = d_ref[0]
    prods = [jnp.dot(d, couple_ref[0, k], preferred_element_type=jnp.float32) for k in range(K)]
    for k in range(K):
        rel, step, slot = peer_place(info, s * K + k)
        slots[(rel + step) * 4 + slot] = prods[k].astype(jnp.bfloat16)

    @pl.when(s == RT - 1)
    def _():
        own_ref[...] = slots[:16]
        cross_ref[...] = slots[16:]


def dense_kernel(info, d_ref, diag_ref, deep_ref, base_ref, back_ref, acc):
    s = pl.program_id(0)

    @pl.when(s == 0)
    def _():
        acc[...] = jnp.zeros_like(acc)

    d = d_ref[0]
    base_ref[0] = lax.dot_general(d, diag_ref[0], NT, preferred_element_type=jnp.float32)
    acc[info[AT_DEEP + s]] += jnp.dot(d, deep_ref[0], preferred_element_type=jnp.float32)

    @pl.when(s == RT - 1)
    def _():
        back_ref[...] = acc[...].astype(jnp.bfloat16)


def pack_kernel(info, table, *rest):
    lines, outs = rest[:4], rest[4:]
    u = along(info)
    for step in range(4):
        for rel in range(2):
            out = outs[rel] if step == 0 else outs[step + 1]
            base = 4 * rel if step else 0
            for e in range(4):
                slot = (u - e) & 3
                tile = asked(info, table, rel, step, slot)

                @pl.when(tile >= 0)
                def _(out=out, base=base, e=e, slot=slot, tile=tile):
                    out[base + slot] = lines[e][tile]


def copies_kernel(moves, sources, *rest):
    refs, sem = rest[:-1], rest[-1]
    started = []
    for i, (src, at, dst, to, count) in enumerate(moves):
        copy = pltpu.make_async_copy(
            refs[src].at[at : at + count], refs[sources + dst].at[to : to + count], sem.at[i]
        )
        copy.start()
        started.append(copy)
    for copy in started:
        copy.wait()


def combine_kernel(info, table, *rest):
    groups, outs, acc = rest[:8], rest[8:12], rest[12]
    step = pl.program_id(0)
    slot = (along(info) + step) & 3
    acc[...] = jnp.zeros_like(acc)
    for e in range(4):
        for rel in range(2):
            tile = asked(info, table, rel, -e, slot)

            @pl.when(tile >= 0)
            def _(g=2 * e + rel, tile=tile):
                acc[tile] += groups[g][0].astype(jnp.float32)

    for e in range(4):

        @pl.when(step == e)
        def _(e=e):
            outs[e][...] = acc[...].astype(jnp.bfloat16)


def below_kernel(info, base_ref, deep_ref, deeper_ref, out_ref):
    s = pl.program_id(0)
    out_ref[0] = base_ref[0] + lax.dot_general(
        deeper_ref[info[AT_DEEP + s]], deep_ref[0], NT, preferred_element_type=jnp.float32
    )


def direct_kernel(info, base_ref, couple_ref, *rest):
    groups, out_ref, slots = rest[:5], rest[5], rest[6]
    s = pl.program_id(0)

    @pl.when(s == 0)
    def _():
        for e in range(4):
            slots[4 * e : 4 * e + 4] = groups[e][...]
        slots[16:] = groups[4][...]

    total = base_ref[0]
    for k in range(K):
        rel, step, slot = peer_place(info, s * K + k)
        got = slots[(rel + ((-step) & 3)) * 4 + slot]
        total += lax.dot_general(got, couple_ref[0, k], NT, preferred_element_type=jnp.float32)
    out_ref[0] = total


def whole(shape):
    return pl.BlockSpec(shape, lambda *a: (0,) * len(shape))


def row(shape):
    return pl.BlockSpec(shape, lambda s, *a: (s,) + (0,) * (len(shape) - 1))


PARAMS = dict(vmem_limit_bytes=20 * 1024 * 1024)
NT = (((1,), (1,)), ((), ()))
LONG = pl.CostEstimate(flops=50_000_000_000, bytes_accessed=100_000_000, transcendentals=0)
COST = pl.CostEstimate(flops=1000, bytes_accessed=1000, transcendentals=0)
GROUP = (4, NV, TD)
PAIR = (8, NV, TD)
HALF = (16, NV, TD)
LINE = (RT, NV, TD)


def bf(shape):
    return jax.ShapeDtypeStruct(shape, jnp.bfloat16)


def products(info, d, couple):
    return pl.pallas_call(
        products_kernel,
        grid_spec=pltpu.PrefetchScalarGridSpec(
            num_scalar_prefetch=1,
            grid=(RT,),
            in_specs=[row((1, NV, TD)), row((1, K, TD, TD))],
            out_specs=[whole(HALF)] * 2,
            scratch_shapes=[pltpu.VMEM((32, NV, TD), jnp.bfloat16)],
        ),
        out_shape=[bf(HALF)] * 2,
        compiler_params=pltpu.CompilerParams(**PARAMS),
        cost_estimate=COST,
        name="products",
    )(info, d, couple)


def dense(info, d, diag, deep):
    return pl.pallas_call(
        dense_kernel,
        grid_spec=pltpu.PrefetchScalarGridSpec(
            num_scalar_prefetch=1,
            grid=(RT,),
            in_specs=[row((1, NV, TD)), row((1, TD, TD)), row((1, TD, TD))],
            out_specs=[row((1, NV, TD)), whole(LINE)],
            scratch_shapes=[pltpu.VMEM(LINE, jnp.float32)],
        ),
        out_shape=[jax.ShapeDtypeStruct(LINE, jnp.float32), bf(LINE)],
        compiler_params=pltpu.CompilerParams(**PARAMS),
        cost_estimate=LONG,
        name="dense",
    )(info, d, diag, deep)


def pack(info, table, lines):
    return pl.pallas_call(
        pack_kernel,
        grid_spec=pltpu.PrefetchScalarGridSpec(
            num_scalar_prefetch=2,
            grid=(1,),
            in_specs=[whole(LINE)] * 4,
            out_specs=[whole(GROUP)] * 2 + [whole(PAIR)] * 3,
        ),
        out_shape=[bf(GROUP)] * 2 + [bf(PAIR)] * 3,
        compiler_params=pltpu.CompilerParams(**PARAMS),
        cost_estimate=COST,
        name="pack",
    )(info, table, *lines)


def copies(arrays, shapes, moves, name):
    anywhere = pl.BlockSpec(memory_space=pl.ANY)
    return pl.pallas_call(
        functools.partial(copies_kernel, moves, len(arrays)),
        in_specs=[anywhere] * len(arrays),
        out_specs=[anywhere] * len(shapes),
        out_shape=[bf(shape) for shape in shapes],
        scratch_shapes=[pltpu.SemaphoreType.DMA((len(moves),))],
        compiler_params=pltpu.CompilerParams(**PARAMS),
        cost_estimate=COST,
        name=name,
    )(*arrays)


def combine(info, table, own, cross, arrived):
    def at(base):
        return pl.BlockSpec(
            (1, NV, TD), lambda step, info, table: (base + ((along(info) + step) & 3), 0, 0)
        )

    args = [own, cross]
    for pair in arrived:
        args += [pair, pair]
    return pl.pallas_call(
        combine_kernel,
        grid_spec=pltpu.PrefetchScalarGridSpec(
            num_scalar_prefetch=2,
            grid=(4,),
            in_specs=[at(0), at(0)] + [at(0), at(4)] * 3,
            out_specs=[whole(LINE)] * 4,
            scratch_shapes=[pltpu.VMEM(LINE, jnp.float32)],
        ),
        out_shape=[bf(LINE)] * 4,
        compiler_params=pltpu.CompilerParams(**PARAMS),
        cost_estimate=COST,
        name="combine",
    )(info, table, *args)


def below(info, base, deep, deeper):
    return pl.pallas_call(
        below_kernel,
        grid_spec=pltpu.PrefetchScalarGridSpec(
            num_scalar_prefetch=1,
            grid=(RT,),
            in_specs=[row((1, NV, TD)), row((1, TD, TD)), whole(LINE)],
            out_specs=row((1, NV, TD)),
        ),
        out_shape=jax.ShapeDtypeStruct(LINE, jnp.float32),
        compiler_params=pltpu.CompilerParams(**PARAMS),
        cost_estimate=COST,
        name="below",
    )(info, base, deep, deeper)


def direct(info, base, couple, groups):
    return pl.pallas_call(
        direct_kernel,
        grid_spec=pltpu.PrefetchScalarGridSpec(
            num_scalar_prefetch=1,
            grid=(RT,),
            in_specs=[row((1, NV, TD)), row((1, K, TD, TD))] + [whole(GROUP)] * 4 + [whole(HALF)],
            out_specs=row((1, NV, TD)),
            scratch_shapes=[pltpu.VMEM((32, NV, TD), jnp.bfloat16)],
        ),
        out_shape=jax.ShapeDtypeStruct(LINE, jnp.float32),
        compiler_params=pltpu.CompilerParams(**PARAMS),
        cost_estimate=COST,
        name="direct",
    )(info, base, couple, *groups)


def local(right_side, diag_tiles, couple_tiles, deep_tiles, peer_col, peer_tile, deep_tile):
    me = lax.axis_index("sub").astype(jnp.int32)
    flat_peer = peer_col.reshape(REFS)
    flat_tile = peer_tile.reshape(REFS)
    coords = jnp.stack([me >> 3, (me >> 1) & 3, me & 1])
    info = jnp.concatenate([flat_peer, coords, deep_tile])
    names = flat_peer[:, None] == jnp.arange(NSUB, dtype=jnp.int32)[None, :]
    want = jnp.sum(jnp.where(names, flat_tile[:, None] + 1, 0), axis=0)
    table = lax.all_to_all(
        jnp.broadcast_to(want[None, :], (NSUB, NSUB)), "sub", split_axis=0, concat_axis=0, tiled=True
    )

    centre = 0.5 * (spectrum_high + spectrum_low)
    spread = 0.5 * (spectrum_high - spectrum_low)
    sigma_ratio = centre / spread
    residual = jnp.swapaxes(right_side, 1, 2)
    direction = residual / centre
    solution = direction
    rho_prev = 1.0 / sigma_ratio
    for sweep in range(CHEB):
        d = direction.astype(jnp.bfloat16)
        lines = [d] + [lax.ppermute(d, "sub", first_axis(e)) for e in (1, 2, 3)]
        deeper = from_behind(d, "slab", -1)
        own, cross = products(info, d, couple_tiles)
        base, deep_back = dense(info, d, diag_tiles, deep_tiles)
        if sweep == 0:
            cross, lines[1:], table = lax.optimization_barrier((cross, lines[1:], table))
        cross = lax.ppermute(cross, "sub", SWAP)
        deep_got = from_behind(deep_back, "slab", 1)
        joined = copies(
            [own, cross],
            [PAIR] * 3,
            [(s, 4 * e, e - 1, 4 * s, 4) for e in (1, 2, 3) for s in (0, 1)],
            "join",
        )
        arrived = [lax.ppermute(joined[e - 1], "sub", second_same(e)) for e in (1, 2, 3)]
        held = (joined, lines[1:], deeper, base)
        unused, lines[1:], deeper, base = lax.optimization_barrier(held)
        near, over, *packed = pack(info, table, lines)
        reached = [lax.ppermute(packed[e - 1], "sub", second_same(e)) for e in (1, 2, 3)]
        sums = combine(info, table, own, cross, arrived)
        owned = [sums[0]] + [lax.ppermute(sums[e], "sub", first_axis(e)) for e in (1, 2, 3)]
        base = below(info, base, deep_tiles, deeper)
        owned, reached, deep_got, base = lax.optimization_barrier((owned, reached, deep_got, base))
        (over,) = copies(
            [over] + reached, [HALF], [(e, 4 * (e > 0), 0, 4 * e, 4) for e in range(4)], "collect"
        )
        over = lax.ppermute(over, "sub", SWAP)
        accum = direct(info, base, couple_tiles, [near] + reached + [over])
        for part in owned + [deep_got]:
            accum = accum + part.astype(jnp.float32)
        residual = residual - accum
        if sweep + 1 < CHEB:
            rho_next = 1.0 / (2.0 * sigma_ratio - rho_prev)
            direction = rho_next * rho_prev * direction + 2.0 * rho_next / spread * residual
            solution = solution + direction
            rho_prev = rho_next
    return (jnp.swapaxes(solution, 1, 2), jnp.swapaxes(residual, 1, 2))


def solution(mesh):
    return jax.shard_map(
        local,
        mesh=mesh,
        in_specs=(
            P(("slab", "sub"), None, None),
            P(("slab", "sub"), None, None),
            P(("slab", "sub"), None, None, None),
            P(("slab", "sub"), None, None),
            P(("slab", "sub"), None),
            P(("slab", "sub"), None),
            P(("slab", "sub")),
        ),
        out_specs=(P(("slab", "sub"), None, None), P(("slab", "sub"), None, None)),
        check_vma=False,
    )
```

```python
import functools

import jax
import jax.numpy as jnp
from jax import lax
from jax.experimental import pallas as pl
from jax.experimental.pallas import tpu as pltpu
from jax.sharding import PartitionSpec as P

CHEB = 3
NX = 4
NY = 4
RT = 5
K = 3
REFS = RT * K
TD = 384
NV = 128
NSUB = 32
AT_X, AT_Y, AT_C, AT_DEEP = REFS, REFS + 1, REFS + 2, REFS + 3

spectrum_low = 0.5
spectrum_high = 6.5


def place(x, y, c):
    return ((x % NX) * NY + (y % NY)) * 2 + c


EVERY = [(x, y, c) for x in range(NX) for y in range(NY) for c in range(2)]


def first_axis(e):
    return [(place(x, y, c), place(x, y + e, 0) if c == 0 else place(x + e, y, 1)) for x, y, c in EVERY]


def second_same(e):
    return [(place(x, y, c), place(x + e, y, 0) if c == 0 else place(x, y + e, 1)) for x, y, c in EVERY]


SWAP = [(place(x, y, c), place(x, y, 1 - c)) for x, y, c in EVERY]


def from_behind(value, axis, by):
    devices = lax.axis_size(axis)
    pairs = [(i, i + by) for i in range(devices) if 0 <= i + by < devices]
    return lax.ppermute(value, axis, pairs)


def peer_place(info, i):
    q = info[i]
    qx, qy, qc = q >> 3, (q >> 1) & 3, q & 1
    even = qc == 0
    step = jnp.where(even, qx - info[AT_X], qy - info[AT_Y]) & 3
    slot = jnp.where(even, qy, qx)
    rel = jnp.where(qc == info[AT_C], 0, 4)
    return rel, step, slot


def along(info):
    return jnp.where(info[AT_C] == 0, info[AT_Y], info[AT_X])


def asked(info, table, rel, step, slot):
    x, y, c = info[AT_X], info[AT_Y], info[AT_C]
    even = c == 0
    px = jnp.where(even, (x + step) & 3, x)
    py = jnp.where(even, y, (y + step) & 3)
    pc = c ^ 1 if rel else c
    ox = jnp.where(even, x, slot)
    oy = jnp.where(even, slot, y)
    return table[(px * NY + py) * 2 + pc, (ox * NY + oy) * 2 + c] - 1


def products_kernel(info, d_ref, couple_ref, own_ref, cross_ref, slots):
    s = pl.program_id(0)
    d = d_ref[0]
    prods = [jnp.dot(d, couple_ref[0, k], preferred_element_type=jnp.float32) for k in range(K)]
    for k in range(K):
        rel, step, slot = peer_place(info, s * K + k)
        slots[(rel + step) * 4 + slot] = prods[k].astype(jnp.bfloat16)

    @pl.when(s == RT - 1)
    def _():
        own_ref[...] = slots[:16]
        cross_ref[...] = slots[16:]


def dense_kernel(info, d_ref, diag_ref, deep_ref, base_ref, back_ref, acc):
    s = pl.program_id(0)

    @pl.when(s == 0)
    def _():
        acc[...] = jnp.zeros_like(acc)

    d = d_ref[0]
    base_ref[0] = lax.dot_general(d, diag_ref[0], NT, preferred_element_type=jnp.float32)
    acc[info[AT_DEEP + s]] += jnp.dot(d, deep_ref[0], preferred_element_type=jnp.float32)

    @pl.when(s == RT - 1)
    def _():
        back_ref[...] = acc[...].astype(jnp.bfloat16)


def pack_kernel(info, table, *rest):
    lines, outs = rest[:4], rest[4:]
    u = along(info)
    for step in range(4):
        for rel in range(2):
            out = outs[rel] if step == 0 else outs[step + 1]
            base = 4 * rel if step else 0
            for e in range(4):
                slot = (u - e) & 3
                tile = asked(info, table, rel, step, slot)

                @pl.when(tile >= 0)
                def _(out=out, base=base, e=e, slot=slot, tile=tile):
                    out[base + slot] = lines[e][tile]


def copies_kernel(moves, sources, *rest):
    refs, sem = rest[:-1], rest[-1]
    started = []
    for i, (src, at, dst, to, count) in enumerate(moves):
        copy = pltpu.make_async_copy(
            refs[src].at[at : at + count], refs[sources + dst].at[to : to + count], sem.at[i]
        )
        copy.start()
        started.append(copy)
    for copy in started:
        copy.wait()


def combine_kernel(info, table, *rest):
    groups, outs, acc = rest[:8], rest[8:12], rest[12]
    step = pl.program_id(0)
    slot = (along(info) + step) & 3
    acc[...] = jnp.zeros_like(acc)
    for e in range(4):
        for rel in range(2):
            tile = asked(info, table, rel, -e, slot)

            @pl.when(tile >= 0)
            def _(g=2 * e + rel, tile=tile):
                acc[tile] += groups[g][0].astype(jnp.float32)

    for e in range(4):

        @pl.when(step == e)
        def _(e=e):
            outs[e][...] = acc[...].astype(jnp.bfloat16)


def below_kernel(info, base_ref, deep_ref, deeper_ref, out_ref):
    s = pl.program_id(0)
    out_ref[0] = base_ref[0] + lax.dot_general(
        deeper_ref[info[AT_DEEP + s]], deep_ref[0], NT, preferred_element_type=jnp.float32
    )


def direct_kernel(info, base_ref, couple_ref, *rest):
    groups, out_ref, slots = rest[:8], rest[8], rest[9]
    s = pl.program_id(0)

    @pl.when(s == 0)
    def _():
        for g in range(8):
            slots[4 * g : 4 * g + 4] = groups[g][...]

    total = base_ref[0]
    for k in range(K):
        rel, step, slot = peer_place(info, s * K + k)
        got = slots[(rel + ((-step) & 3)) * 4 + slot]
        total += lax.dot_general(got, couple_ref[0, k], NT, preferred_element_type=jnp.float32)
    out_ref[0] = total


def whole(shape):
    return pl.BlockSpec(shape, lambda *a: (0,) * len(shape))


def row(shape):
    return pl.BlockSpec(shape, lambda s, *a: (s,) + (0,) * (len(shape) - 1))


PARAMS = dict(vmem_limit_bytes=20 * 1024 * 1024)
NT = (((1,), (1,)), ((), ()))
LONG = pl.CostEstimate(flops=50_000_000_000, bytes_accessed=100_000_000, transcendentals=0)
COST = pl.CostEstimate(flops=1000, bytes_accessed=1000, transcendentals=0)
GROUP = (4, NV, TD)
PAIR = (8, NV, TD)
HALF = (16, NV, TD)
LINE = (RT, NV, TD)


def bf(shape):
    return jax.ShapeDtypeStruct(shape, jnp.bfloat16)


def products(info, d, couple):
    return pl.pallas_call(
        products_kernel,
        grid_spec=pltpu.PrefetchScalarGridSpec(
            num_scalar_prefetch=1,
            grid=(RT,),
            in_specs=[row((1, NV, TD)), row((1, K, TD, TD))],
            out_specs=[whole(HALF)] * 2,
            scratch_shapes=[pltpu.VMEM((32, NV, TD), jnp.bfloat16)],
        ),
        out_shape=[bf(HALF)] * 2,
        compiler_params=pltpu.CompilerParams(**PARAMS),
        cost_estimate=COST,
        name="products",
    )(info, d, couple)


def dense(info, d, diag, deep):
    return pl.pallas_call(
        dense_kernel,
        grid_spec=pltpu.PrefetchScalarGridSpec(
            num_scalar_prefetch=1,
            grid=(RT,),
            in_specs=[row((1, NV, TD)), row((1, TD, TD)), row((1, TD, TD))],
            out_specs=[row((1, NV, TD)), whole(LINE)],
            scratch_shapes=[pltpu.VMEM(LINE, jnp.float32)],
        ),
        out_shape=[jax.ShapeDtypeStruct(LINE, jnp.float32), bf(LINE)],
        compiler_params=pltpu.CompilerParams(**PARAMS),
        cost_estimate=LONG,
        name="dense",
    )(info, d, diag, deep)


def pack(info, table, lines):
    return pl.pallas_call(
        pack_kernel,
        grid_spec=pltpu.PrefetchScalarGridSpec(
            num_scalar_prefetch=2,
            grid=(1,),
            in_specs=[whole(LINE)] * 4,
            out_specs=[whole(GROUP)] * 2 + [whole(PAIR)] * 3,
        ),
        out_shape=[bf(GROUP)] * 2 + [bf(PAIR)] * 3,
        compiler_params=pltpu.CompilerParams(**PARAMS),
        cost_estimate=COST,
        name="pack",
    )(info, table, *lines)


def copies(arrays, shapes, moves, name):
    anywhere = pl.BlockSpec(memory_space=pl.ANY)
    return pl.pallas_call(
        functools.partial(copies_kernel, moves, len(arrays)),
        in_specs=[anywhere] * len(arrays),
        out_specs=[anywhere] * len(shapes),
        out_shape=[bf(shape) for shape in shapes],
        scratch_shapes=[pltpu.SemaphoreType.DMA((len(moves),))],
        compiler_params=pltpu.CompilerParams(**PARAMS),
        cost_estimate=COST,
        name=name,
    )(*arrays)


def combine(info, table, own, cross, arrived):
    def at(base):
        return pl.BlockSpec(
            (1, NV, TD), lambda step, info, table: (base + ((along(info) + step) & 3), 0, 0)
        )

    args = [own, cross]
    for pair in arrived:
        args += [pair, pair]
    return pl.pallas_call(
        combine_kernel,
        grid_spec=pltpu.PrefetchScalarGridSpec(
            num_scalar_prefetch=2,
            grid=(4,),
            in_specs=[at(0), at(0)] + [at(0), at(4)] * 3,
            out_specs=[whole(LINE)] * 4,
            scratch_shapes=[pltpu.VMEM(LINE, jnp.float32)],
        ),
        out_shape=[bf(LINE)] * 4,
        compiler_params=pltpu.CompilerParams(**PARAMS),
        cost_estimate=COST,
        name="combine",
    )(info, table, *args)


def below(info, base, deep, deeper):
    return pl.pallas_call(
        below_kernel,
        grid_spec=pltpu.PrefetchScalarGridSpec(
            num_scalar_prefetch=1,
            grid=(RT,),
            in_specs=[row((1, NV, TD)), row((1, TD, TD)), whole(LINE)],
            out_specs=row((1, NV, TD)),
        ),
        out_shape=jax.ShapeDtypeStruct(LINE, jnp.float32),
        compiler_params=pltpu.CompilerParams(**PARAMS),
        cost_estimate=COST,
        name="below",
    )(info, base, deep, deeper)


def direct(info, base, couple, groups):
    return pl.pallas_call(
        direct_kernel,
        grid_spec=pltpu.PrefetchScalarGridSpec(
            num_scalar_prefetch=1,
            grid=(RT,),
            in_specs=[row((1, NV, TD)), row((1, K, TD, TD))] + [whole(GROUP)] * 8,
            out_specs=row((1, NV, TD)),
            scratch_shapes=[pltpu.VMEM((32, NV, TD), jnp.bfloat16)],
        ),
        out_shape=jax.ShapeDtypeStruct(LINE, jnp.float32),
        compiler_params=pltpu.CompilerParams(**PARAMS),
        cost_estimate=COST,
        name="direct",
    )(info, base, couple, *groups)


def local(right_side, diag_tiles, couple_tiles, deep_tiles, peer_col, peer_tile, deep_tile):
    me = lax.axis_index("sub").astype(jnp.int32)
    flat_peer = peer_col.reshape(REFS)
    flat_tile = peer_tile.reshape(REFS)
    coords = jnp.stack([me >> 3, (me >> 1) & 3, me & 1])
    info = jnp.concatenate([flat_peer, coords, deep_tile])
    names = flat_peer[:, None] == jnp.arange(NSUB, dtype=jnp.int32)[None, :]
    want = jnp.sum(jnp.where(names, flat_tile[:, None] + 1, 0), axis=0)
    table = lax.all_to_all(
        jnp.broadcast_to(want[None, :], (NSUB, NSUB)), "sub", split_axis=0, concat_axis=0, tiled=True
    )

    centre = 0.5 * (spectrum_high + spectrum_low)
    spread = 0.5 * (spectrum_high - spectrum_low)
    sigma_ratio = centre / spread
    residual = jnp.swapaxes(right_side, 1, 2)
    direction = residual / centre
    solution = direction
    rho_prev = 1.0 / sigma_ratio
    for sweep in range(CHEB):
        d = direction.astype(jnp.bfloat16)
        lines = [d] + [lax.ppermute(d, "sub", first_axis(e)) for e in (1, 2, 3)]
        deeper = from_behind(d, "slab", -1)
        own, cross = products(info, d, couple_tiles)
        base, deep_back = dense(info, d, diag_tiles, deep_tiles)
        if sweep == 0:
            cross, lines[1:], table = lax.optimization_barrier((cross, lines[1:], table))
        cross = lax.ppermute(cross, "sub", SWAP)
        deep_got = from_behind(deep_back, "slab", 1)
        joined = copies(
            [own, cross],
            [PAIR] * 3,
            [(s, 4 * e, e - 1, 4 * s, 4) for e in (1, 2, 3) for s in (0, 1)],
            "join",
        )
        arrived = [lax.ppermute(joined[e - 1], "sub", second_same(e)) for e in (1, 2, 3)]
        held = (joined, lines[1:], deeper, base)
        unused, lines[1:], deeper, base = lax.optimization_barrier(held)
        near, over, *packed = pack(info, table, lines)
        reached = [lax.ppermute(packed[e - 1], "sub", second_same(e)) for e in (1, 2, 3)]
        sums = combine(info, table, own, cross, arrived)
        owned = [sums[0]] + [lax.ppermute(sums[e], "sub", first_axis(e)) for e in (1, 2, 3)]
        base = below(info, base, deep_tiles, deeper)
        over = lax.ppermute(over, "sub", SWAP)
        held = (owned[2], reached, deep_got, base, over)
        owned[2], reached, deep_got, base, over = lax.optimization_barrier(held)
        overs = [over] + [lax.ppermute(tiles[4:], "sub", SWAP) for tiles in reached]
        accum = direct(info, base, couple_tiles, [near] + reached + overs)
        for part in owned + [deep_got]:
            accum = accum + part.astype(jnp.float32)
        residual = residual - accum
        if sweep + 1 < CHEB:
            rho_next = 1.0 / (2.0 * sigma_ratio - rho_prev)
            direction = rho_next * rho_prev * direction + 2.0 * rho_next / spread * residual
            solution = solution + direction
            rho_prev = rho_next
    return (jnp.swapaxes(solution, 1, 2), jnp.swapaxes(residual, 1, 2))


def solution(mesh):
    return jax.shard_map(
        local,
        mesh=mesh,
        in_specs=(
            P(("slab", "sub"), None, None),
            P(("slab", "sub"), None, None),
            P(("slab", "sub"), None, None, None),
            P(("slab", "sub"), None, None),
            P(("slab", "sub"), None),
            P(("slab", "sub"), None),
            P(("slab", "sub")),
        ),
        out_specs=(P(("slab", "sub"), None, None), P(("slab", "sub"), None, None)),
        check_vma=False,
    )
```

```python
import functools

import jax
import jax.numpy as jnp
from jax import lax
from jax.experimental import pallas as pl
from jax.experimental.pallas import tpu as pltpu
from jax.sharding import PartitionSpec as P

CHEB = 3
NX = 4
NY = 4
RT = 5
K = 3
REFS = RT * K
TD = 384
NV = 128
NSUB = 32
AT_X, AT_Y, AT_C, AT_DEEP = REFS, REFS + 1, REFS + 2, REFS + 3

spectrum_low = 0.5
spectrum_high = 6.5


def place(x, y, c):
    return ((x % NX) * NY + (y % NY)) * 2 + c


EVERY = [(x, y, c) for x in range(NX) for y in range(NY) for c in range(2)]


def first_axis(e):
    return [(place(x, y, c), place(x, y + e, 0) if c == 0 else place(x + e, y, 1)) for x, y, c in EVERY]


def second_same(e):
    return [(place(x, y, c), place(x + e, y, 0) if c == 0 else place(x, y + e, 1)) for x, y, c in EVERY]


SWAP = [(place(x, y, c), place(x, y, 1 - c)) for x, y, c in EVERY]


def from_behind(value, axis, by):
    devices = lax.axis_size(axis)
    pairs = [(i, i + by) for i in range(devices) if 0 <= i + by < devices]
    return lax.ppermute(value, axis, pairs)


def peer_place(info, i):
    q = info[i]
    qx, qy, qc = q >> 3, (q >> 1) & 3, q & 1
    even = qc == 0
    step = jnp.where(even, qx - info[AT_X], qy - info[AT_Y]) & 3
    slot = jnp.where(even, qy, qx)
    rel = jnp.where(qc == info[AT_C], 0, 4)
    return rel, step, slot


def along(info):
    return jnp.where(info[AT_C] == 0, info[AT_Y], info[AT_X])


def asked(info, table, rel, step, slot):
    x, y, c = info[AT_X], info[AT_Y], info[AT_C]
    even = c == 0
    px = jnp.where(even, (x + step) & 3, x)
    py = jnp.where(even, y, (y + step) & 3)
    pc = c ^ 1 if rel else c
    ox = jnp.where(even, x, slot)
    oy = jnp.where(even, slot, y)
    return table[(px * NY + py) * 2 + pc, (ox * NY + oy) * 2 + c] - 1


def products_kernel(info, d_ref, couple_ref, own_ref, cross_ref):
    s = pl.program_id(0)
    d = d_ref[0]
    prods = [jnp.dot(d, couple_ref[0, k], preferred_element_type=jnp.float32) for k in range(K)]
    for k in range(K):
        rel, step, slot = peer_place(info, s * K + k)
        at = step * 4 + slot
        tile = prods[k].astype(jnp.bfloat16)
        own_ref[at] = jnp.where(rel == 0, tile, own_ref[at])
        cross_ref[at] = jnp.where(rel == 0, cross_ref[at], tile)


def dense_kernel(info, d_ref, diag_ref, deep_ref, base_ref, back_ref, acc):
    s = pl.program_id(0)

    @pl.when(s == 0)
    def _():
        acc[...] = jnp.zeros_like(acc)

    d = d_ref[0]
    base_ref[0] = lax.dot_general(d, diag_ref[0], NT, preferred_element_type=jnp.float32)
    acc[info[AT_DEEP + s]] += jnp.dot(d, deep_ref[0], preferred_element_type=jnp.float32)

    @pl.when(s == RT - 1)
    def _():
        back_ref[...] = acc[...].astype(jnp.bfloat16)


def pack_kernel(info, table, *rest):
    lines, outs = rest[:4], rest[4:]
    u = along(info)
    for step in range(4):
        for rel in range(2):
            out = outs[rel] if step == 0 else outs[step + 1]
            base = 4 * rel if step else 0
            for e in range(4):
                slot = (u - e) & 3
                tile = asked(info, table, rel, step, slot)

                @pl.when(tile >= 0)
                def _(out=out, base=base, e=e, slot=slot, tile=tile):
                    out[base + slot] = lines[e][tile]


def copies_kernel(moves, sources, *rest):
    refs, sem = rest[:-1], rest[-1]
    started = []
    for i, (src, at, dst, to, count) in enumerate(moves):
        copy = pltpu.make_async_copy(
            refs[src].at[at : at + count], refs[sources + dst].at[to : to + count], sem.at[i]
        )
        copy.start()
        started.append(copy)
    for copy in started:
        copy.wait()


def combine_kernel(info, table, *rest):
    groups, outs, acc = rest[:8], rest[8:12], rest[12]
    step = pl.program_id(0)
    slot = (along(info) + step) & 3
    acc[...] = jnp.zeros_like(acc)
    for e in range(4):
        for rel in range(2):
            tile = asked(info, table, rel, -e, slot)

            @pl.when(tile >= 0)
            def _(g=2 * e + rel, tile=tile):
                acc[tile] += groups[g][0].astype(jnp.float32)

    for e in range(4):

        @pl.when(step == e)
        def _(e=e):
            outs[e][...] = acc[...].astype(jnp.bfloat16)


def below_kernel(info, base_ref, deep_ref, deeper_ref, out_ref):
    s = pl.program_id(0)
    out_ref[0] = base_ref[0] + lax.dot_general(
        deeper_ref[info[AT_DEEP + s]], deep_ref[0], NT, preferred_element_type=jnp.float32
    )


def direct_kernel(info, base_ref, couple_ref, *rest):
    groups, out_ref, slots = rest[:8], rest[8], rest[9]
    s = pl.program_id(0)

    @pl.when(s == 0)
    def _():
        for g in range(8):
            slots[4 * g : 4 * g + 4] = groups[g][...]

    total = base_ref[0]
    for k in range(K):
        rel, step, slot = peer_place(info, s * K + k)
        got = slots[(rel + ((-step) & 3)) * 4 + slot]
        total += lax.dot_general(got, couple_ref[0, k], NT, preferred_element_type=jnp.float32)
    out_ref[0] = total


def whole(shape):
    return pl.BlockSpec(shape, lambda *a: (0,) * len(shape))


def row(shape):
    return pl.BlockSpec(shape, lambda s, *a: (s,) + (0,) * (len(shape) - 1))


PARAMS = dict(vmem_limit_bytes=20 * 1024 * 1024)
NT = (((1,), (1,)), ((), ()))
LONG = pl.CostEstimate(flops=50_000_000_000, bytes_accessed=100_000_000, transcendentals=0)
COST = pl.CostEstimate(flops=1000, bytes_accessed=1000, transcendentals=0)
GROUP = (4, NV, TD)
PAIR = (8, NV, TD)
HALF = (16, NV, TD)
LINE = (RT, NV, TD)


def bf(shape):
    return jax.ShapeDtypeStruct(shape, jnp.bfloat16)


def products(info, d, couple):
    return pl.pallas_call(
        products_kernel,
        grid_spec=pltpu.PrefetchScalarGridSpec(
            num_scalar_prefetch=1,
            grid=(RT,),
            in_specs=[row((1, NV, TD)), row((1, K, TD, TD))],
            out_specs=[whole(HALF)] * 2,
        ),
        out_shape=[bf(HALF)] * 2,
        compiler_params=pltpu.CompilerParams(**PARAMS),
        cost_estimate=COST,
        name="products",
    )(info, d, couple)


def dense(info, d, diag, deep):
    return pl.pallas_call(
        dense_kernel,
        grid_spec=pltpu.PrefetchScalarGridSpec(
            num_scalar_prefetch=1,
            grid=(RT,),
            in_specs=[row((1, NV, TD)), row((1, TD, TD)), row((1, TD, TD))],
            out_specs=[row((1, NV, TD)), whole(LINE)],
            scratch_shapes=[pltpu.VMEM(LINE, jnp.float32)],
        ),
        out_shape=[jax.ShapeDtypeStruct(LINE, jnp.float32), bf(LINE)],
        compiler_params=pltpu.CompilerParams(**PARAMS),
        cost_estimate=LONG,
        name="dense",
    )(info, d, diag, deep)


def pack(info, table, lines):
    return pl.pallas_call(
        pack_kernel,
        grid_spec=pltpu.PrefetchScalarGridSpec(
            num_scalar_prefetch=2,
            grid=(1,),
            in_specs=[whole(LINE)] * 4,
            out_specs=[whole(GROUP)] * 2 + [whole(PAIR)] * 3,
        ),
        out_shape=[bf(GROUP)] * 2 + [bf(PAIR)] * 3,
        compiler_params=pltpu.CompilerParams(**PARAMS),
        cost_estimate=COST,
        name="pack",
    )(info, table, *lines)


def copies(arrays, shapes, moves, name):
    anywhere = pl.BlockSpec(memory_space=pl.ANY)
    return pl.pallas_call(
        functools.partial(copies_kernel, moves, len(arrays)),
        in_specs=[anywhere] * len(arrays),
        out_specs=[anywhere] * len(shapes),
        out_shape=[bf(shape) for shape in shapes],
        scratch_shapes=[pltpu.SemaphoreType.DMA((len(moves),))],
        compiler_params=pltpu.CompilerParams(**PARAMS),
        cost_estimate=COST,
        name=name,
    )(*arrays)


def combine(info, table, own, cross, arrived):
    def at(base):
        return pl.BlockSpec(
            (1, NV, TD), lambda step, info, table: (base + ((along(info) + step) & 3), 0, 0)
        )

    args = [own, cross]
    for pair in arrived:
        args += [pair, pair]
    return pl.pallas_call(
        combine_kernel,
        grid_spec=pltpu.PrefetchScalarGridSpec(
            num_scalar_prefetch=2,
            grid=(4,),
            in_specs=[at(0), at(0)] + [at(0), at(4)] * 3,
            out_specs=[whole(LINE)] * 4,
            scratch_shapes=[pltpu.VMEM(LINE, jnp.float32)],
        ),
        out_shape=[bf(LINE)] * 4,
        compiler_params=pltpu.CompilerParams(**PARAMS),
        cost_estimate=COST,
        name="combine",
    )(info, table, *args)


def below(info, base, deep, deeper):
    return pl.pallas_call(
        below_kernel,
        grid_spec=pltpu.PrefetchScalarGridSpec(
            num_scalar_prefetch=1,
            grid=(RT,),
            in_specs=[row((1, NV, TD)), row((1, TD, TD)), whole(LINE)],
            out_specs=row((1, NV, TD)),
        ),
        out_shape=jax.ShapeDtypeStruct(LINE, jnp.float32),
        compiler_params=pltpu.CompilerParams(**PARAMS),
        cost_estimate=COST,
        name="below",
    )(info, base, deep, deeper)


def direct(info, base, couple, groups):
    return pl.pallas_call(
        direct_kernel,
        grid_spec=pltpu.PrefetchScalarGridSpec(
            num_scalar_prefetch=1,
            grid=(RT,),
            in_specs=[row((1, NV, TD)), row((1, K, TD, TD))] + [whole(GROUP)] * 8,
            out_specs=row((1, NV, TD)),
            scratch_shapes=[pltpu.VMEM((32, NV, TD), jnp.bfloat16)],
        ),
        out_shape=jax.ShapeDtypeStruct(LINE, jnp.float32),
        compiler_params=pltpu.CompilerParams(**PARAMS),
        cost_estimate=COST,
        name="direct",
    )(info, base, couple, *groups)


def local(right_side, diag_tiles, couple_tiles, deep_tiles, peer_col, peer_tile, deep_tile):
    me = lax.axis_index("sub").astype(jnp.int32)
    flat_peer = peer_col.reshape(REFS)
    flat_tile = peer_tile.reshape(REFS)
    coords = jnp.stack([me >> 3, (me >> 1) & 3, me & 1])
    info = jnp.concatenate([flat_peer, coords, deep_tile])
    names = flat_peer[:, None] == jnp.arange(NSUB, dtype=jnp.int32)[None, :]
    want = jnp.sum(jnp.where(names, flat_tile[:, None] + 1, 0), axis=0)
    table = lax.all_to_all(
        jnp.broadcast_to(want[None, :], (NSUB, NSUB)), "sub", split_axis=0, concat_axis=0, tiled=True
    )

    centre = 0.5 * (spectrum_high + spectrum_low)
    spread = 0.5 * (spectrum_high - spectrum_low)
    sigma_ratio = centre / spread
    residual = jnp.swapaxes(right_side, 1, 2)
    direction = residual / centre
    solution = direction
    rho_prev = 1.0 / sigma_ratio
    for sweep in range(CHEB):
        d = direction.astype(jnp.bfloat16)
        lines = [d] + [lax.ppermute(d, "sub", first_axis(e)) for e in (1, 2, 3)]
        deeper = from_behind(d, "slab", -1)
        own, cross = products(info, d, couple_tiles)
        base, deep_back = dense(info, d, diag_tiles, deep_tiles)
        if sweep == 0:
            cross, lines[1:], table = lax.optimization_barrier((cross, lines[1:], table))
        cross = lax.ppermute(cross, "sub", SWAP)
        deep_got = from_behind(deep_back, "slab", 1)
        joined = copies(
            [own, cross],
            [PAIR] * 3,
            [(s, 4 * e, e - 1, 4 * s, 4) for e in (1, 2, 3) for s in (0, 1)],
            "join",
        )
        arrived = [lax.ppermute(joined[e - 1], "sub", second_same(e)) for e in (1, 2, 3)]
        held = (joined, lines[1:], deeper, base)
        unused, lines[1:], deeper, base = lax.optimization_barrier(held)
        near, over, *packed = pack(info, table, lines)
        reached = [lax.ppermute(packed[e - 1], "sub", second_same(e)) for e in (1, 2, 3)]
        sums = combine(info, table, own, cross, arrived)
        owned = [sums[0]] + [lax.ppermute(sums[e], "sub", first_axis(e)) for e in (1, 2, 3)]
        base = below(info, base, deep_tiles, deeper)
        over = lax.ppermute(over, "sub", SWAP)
        held = (owned[2], reached, deep_got, base, over)
        owned[2], reached, deep_got, base, over = lax.optimization_barrier(held)
        overs = [over] + [lax.ppermute(tiles[4:], "sub", SWAP) for tiles in reached]
        accum = direct(info, base, couple_tiles, [near] + reached + overs)
        for part in owned + [deep_got]:
            accum = accum + part.astype(jnp.float32)
        residual = residual - accum
        if sweep + 1 < CHEB:
            rho_next = 1.0 / (2.0 * sigma_ratio - rho_prev)
            direction = rho_next * rho_prev * direction + 2.0 * rho_next / spread * residual
            solution = solution + direction
            rho_prev = rho_next
    return (jnp.swapaxes(solution, 1, 2), jnp.swapaxes(residual, 1, 2))


def solution(mesh):
    return jax.shard_map(
        local,
        mesh=mesh,
        in_specs=(
            P(("slab", "sub"), None, None),
            P(("slab", "sub"), None, None),
            P(("slab", "sub"), None, None, None),
            P(("slab", "sub"), None, None),
            P(("slab", "sub"), None),
            P(("slab", "sub"), None),
            P(("slab", "sub")),
        ),
        out_specs=(P(("slab", "sub"), None, None), P(("slab", "sub"), None, None)),
        check_vma=False,
    )
```
